512 devices in a mesh: gx: 32 (over x, z), gy: 16 (over y, core).
Axes of the slice: x: 4, y: 8, z: 8, core: 2. Of those that a mesh axis runs over, the one named last changes fastest.
Arguments:
- forcing_terms: float32 [32, 16, 64, 512], P('gx', 'gy'), may hold values from -6 to 6
- schur: bfloat16 [32, 16, 1024, 1024], P('gx', 'gy'), as said below
- flexibility: bfloat16 [32, 16, 1024, 1024], P('gx', 'gy'), as said below
- coarse_modes: float32 [32, 16, 8, 512], P('gx', 'gy'), may hold values from -1.2 to 1.2
- coarse_map: int32 [32, 16, 8], P('gx', 'gy'), may hold values from 0 to 511, as said below
- face_slot_count: int32 [32, 16, 2], P('gx', 'gy'), may hold values from 128 to 256, as said below
- coarse_inverse: bfloat16 [512, 512], replicated, as said below
Outputs:
- multipliers: float32 [32, 16, 64, 512], P('gx', 'gy')
- residual: float32 [32, 16, 64, 512], P('gx', 'gy')
The draws below stay inside these ranges and needn't reach their ends.
Inputs may be any that keep to these rules, and one draw needn't show every extreme that they name: coarse_map[s, c, k] = min(s + a, 31) * 16 + min(c + b, 15) with a and b each 0 or 1, both 0 for k = 0. `face_slot_count`: some face in every draw has exactly 256 live slots. `schur`: symmetric positive definite. `flexibility`: symmetric positive definite. `coarse_inverse`: symmetric positive definite.
All inputs are finite; a program needn't handle non-finite values.
Results may differ from the reference program's by a relative error of at most 0.0043.
Values may be sent and summed in bfloat16 or wider, within the bound.
A program may use at most 64 MiB of HBM per device.

```python
import math
import jax
import jax.numpy as jnp
from jax import lax

FACE_DOFS = 256
NB = 1024
RHS = 64
KC = 8
ITERS = 2
SLAB_TOTAL = 32
COLUMN_TOTAL = 16
NCOARSE = 512


def spd_blocks(key, spectrum, count, stretch, out_type):
    key_perm, key_scale = jax.random.split(key, 2)
    groups = spectrum.shape[0]
    freq = jnp.arange(count, dtype=jnp.int32)
    folded = jnp.minimum(freq, count - freq)
    full = spectrum[:, folded]
    phase = freq[:, None] * freq[None, :] % count
    table = jnp.cos(phase.astype(jnp.float32) * (2.0 * math.pi / count))
    coeffs = jnp.dot(full, table, precision=lax.Precision.HIGHEST) / count
    perm_keys = jax.random.split(key_perm, groups)

    def permute(single_key):
        return jax.random.permutation(single_key, count).astype(jnp.int32)
    perms = jax.vmap(permute)(perm_keys)
    scales = jnp.exp(stretch * (jax.random.uniform(key_scale, (groups, count), jnp.float32) - 0.5))

    def one_matrix(operands):
        values, order, factors = operands
        distance = (order[:, None] - order[None, :]) % count
        distance = jnp.minimum(distance, count - distance)
        outer = factors[:, None] * factors[None, :]
        return (values[distance] * outer).astype(out_type)
    return lax.map(one_matrix, (coeffs, perms, scales))


def draw_schur(key, part):
    key = jax.random.fold_in(key, 3)
    key_spec, key_rest = jax.random.split(key, 2)
    unit = jax.random.uniform(key_spec, (SLAB_TOTAL * COLUMN_TOTAL, NB // 2 + 1), jnp.float32)
    spectrum = 0.6 * jnp.exp(unit * math.log(4.0 / 0.6))
    stretch = 0.7
    blocks = spd_blocks(key_rest, spectrum, NB, stretch, jnp.bfloat16)
    return blocks.reshape(SLAB_TOTAL, COLUMN_TOTAL, NB, NB)


def draw_flexibility(key, part):
    key = jax.random.fold_in(key, 5)
    key_spec, key_rest = jax.random.split(key, 2)
    unit = jax.random.uniform(key_spec, (SLAB_TOTAL * COLUMN_TOTAL, NB // 2 + 1), jnp.float32)
    spectrum = 0.5 * jnp.exp(unit * math.log(3.0 / 0.5))
    stretch = 0.7
    blocks = spd_blocks(key_rest, spectrum, NB, stretch, jnp.bfloat16)
    return blocks.reshape(SLAB_TOTAL, COLUMN_TOTAL, NB, NB)


def draw_coarse_inverse(key, part):
    key = jax.random.fold_in(key, 9)
    key_spec, key_rest = jax.random.split(key, 2)
    unit = jax.random.uniform(key_spec, (1, NCOARSE // 2 + 1), jnp.float32)
    spectrum = 0.15 * jnp.exp(unit * math.log(6.0))
    stretch = 0.7
    weight = 2.0
    rough = spd_blocks(key_rest, spectrum, NCOARSE, stretch, jnp.float32)[0]
    places = jnp.arange(NCOARSE, dtype=jnp.int32)
    slab_place = (places // COLUMN_TOTAL).astype(jnp.float32)
    column_place = (places % COLUMN_TOTAL).astype(jnp.float32)
    reach_slab = max(SLAB_TOTAL / 2.0, 1.0)
    reach_column = max(COLUMN_TOTAL / 2.0, 1.0)
    slab_gap = jnp.abs(slab_place[:, None] - slab_place[None, :]) / reach_slab
    column_gap = jnp.abs(column_place[:, None] - column_place[None, :]) / reach_column
    kernel = jnp.exp(-(slab_gap + column_gap))
    return (rough + weight / math.sqrt(NCOARSE) * kernel).astype(jnp.bfloat16)


def draw_coarse_map(key, part):
    key = jax.random.fold_in(key, 7)
    offsets = jax.random.randint(key, (SLAB_TOTAL, COLUMN_TOTAL, KC, 2), 0, 2, dtype=jnp.int32)
    first = (jnp.arange(KC, dtype=jnp.int32) == 0)[None, None, :, None]
    offsets = jnp.where(first, 0, offsets)
    slab_index = jnp.arange(SLAB_TOTAL, dtype=jnp.int32)[:, None, None]
    column_index = jnp.arange(COLUMN_TOTAL, dtype=jnp.int32)[None, :, None]
    vertex_slab = jnp.minimum(slab_index + offsets[..., 0], SLAB_TOTAL - 1)
    vertex_column = jnp.minimum(column_index + offsets[..., 1], COLUMN_TOTAL - 1)
    return (vertex_slab * COLUMN_TOTAL + vertex_column).astype(jnp.int32)


def draw_face_slot_count(key, part):
    key = jax.random.fold_in(key, 11)
    key_len, key_top, key_low = jax.random.split(key, 3)
    count = SLAB_TOTAL * COLUMN_TOTAL * 2
    lengths = jax.random.randint(key_len, (count,), FACE_DOFS // 2, FACE_DOFS + 1, dtype=jnp.int32)
    top = jax.random.randint(key_top, (), 0, count, dtype=jnp.int32)
    low = (top + 1 + jax.random.randint(key_low, (), 0, count - 1, dtype=jnp.int32)) % count
    places = jnp.arange(count, dtype=jnp.int32)
    lengths = jnp.where(places == top, FACE_DOFS, lengths)
    lengths = jnp.where(places == low, FACE_DOFS // 2, lengths)
    return lengths.reshape(SLAB_TOTAL, COLUMN_TOTAL, 2)


def level_of(own_key, shape, pieces, least, largest):
    loudness = 1.0
    for axis_at, parts in pieces:
        heights = jax.random.uniform(jax.random.fold_in(jax.random.fold_in(own_key, 6), axis_at), (parts,), jnp.float32, least / len(pieces), largest / len(pieces))
        loudness = loudness * jnp.repeat(jnp.exp(heights), shape[axis_at] // parts).reshape((-1,) + (1,) * (len(shape) - 1 - axis_at))
    return loudness


def noise(key, shape, width, reach, shards=(), kind=jnp.bfloat16):
    entries = width * jax.random.normal(key, shape, jnp.float32)
    if shards:
        entries = entries * level_of(key, shape, shards, -0.22, 0.18)
    return jnp.clip(entries, -reach, reach).astype(kind)


def setup_inputs(seed: int = 0) -> dict:
    key_list = jax.random.split(jax.random.key(seed), 8)
    forcing_terms = noise(key_list[0], (SLAB_TOTAL, COLUMN_TOTAL, RHS, 2 * FACE_DOFS), 1.0, 6.0, ((0, 32), (1, 16)), jnp.float32)
    schur = draw_schur(jax.random.fold_in(key_list[7], 71), 0)
    flexibility = draw_flexibility(jax.random.fold_in(key_list[7], 71), 0)
    coarse_modes = noise(key_list[3], (SLAB_TOTAL, COLUMN_TOTAL, KC, 2 * FACE_DOFS), 0.2, 1.2, ((0, 32), (1, 16)), jnp.float32)
    coarse_map = draw_coarse_map(jax.random.fold_in(key_list[7], 71), 0)
    face_slot_count = draw_face_slot_count(jax.random.fold_in(key_list[7], 71), 0)
    coarse_inverse = draw_coarse_inverse(jax.random.fold_in(key_list[7], 71), 0)
    return {"forcing_terms": forcing_terms, "schur": schur, "flexibility": flexibility, "coarse_modes": coarse_modes, "coarse_map": coarse_map, "face_slot_count": face_slot_count, "coarse_inverse": coarse_inverse}


highest = lax.Precision.HIGHEST


def active_mask(face_slot_count):
    positions = jnp.arange(FACE_DOFS, dtype=jnp.int32)
    interior_flag = positions[None, None, None, :] < face_slot_count[:, :, :, None]
    slab_ok = jnp.broadcast_to((jnp.arange(SLAB_TOTAL, dtype=jnp.int32) < SLAB_TOTAL - 1)[:, None], (SLAB_TOTAL, COLUMN_TOTAL))
    column_ok = jnp.broadcast_to((jnp.arange(COLUMN_TOTAL, dtype=jnp.int32) < COLUMN_TOTAL - 1)[None, :], (SLAB_TOTAL, COLUMN_TOTAL))
    edge_valid = jnp.stack([slab_ok, column_ok], axis=2)
    slot_activity = jnp.logical_and(interior_flag, edge_valid[:, :, :, None])
    return slot_activity.reshape(SLAB_TOTAL, COLUMN_TOTAL, 1, 2 * FACE_DOFS).astype(jnp.float32)


def distribute_values(multiplier_vector):
    face_x = multiplier_vector[..., :FACE_DOFS]
    face_y = multiplier_vector[..., FACE_DOFS:]
    below_x = jnp.concatenate([jnp.zeros_like(face_x[:1]), face_x[:-1]], axis=0)
    below_y = jnp.concatenate([jnp.zeros_like(face_y[:, :1]), face_y[:, :-1]], axis=1)
    return jnp.concatenate([-below_x, face_x, -below_y, face_y], axis=-1).astype(jnp.bfloat16)


def gather_owned(operator_images, slot_activity):
    minus_x = operator_images[..., :FACE_DOFS]
    forward_shift_x = operator_images[..., FACE_DOFS:2 * FACE_DOFS]
    minus_y = operator_images[..., 2 * FACE_DOFS:3 * FACE_DOFS]
    forward_shift_y = operator_images[..., 3 * FACE_DOFS:]
    upper_neighbour_x = jnp.concatenate([minus_x[1:], jnp.zeros_like(minus_x[:1])], axis=0)
    upper_neighbour_y = jnp.concatenate([minus_y[:, 1:], jnp.zeros_like(minus_y[:, :1])], axis=1)
    return slot_activity * jnp.concatenate([forward_shift_x - upper_neighbour_x, forward_shift_y - upper_neighbour_y], axis=-1)


def subdomain_products(halves, matrices):
    def per_slab(operands):
        slab_rows, slab_mats = operands
        return jnp.einsum("crk,ckj->crj", slab_rows.astype(jnp.float32), slab_mats.astype(jnp.float32))
    return lax.map(per_slab, (halves, matrices))


def coarse_term(multiplier_vector, filtered_modes, coarse_map, coarse_inverse):
    local_terms = jnp.einsum("scrf,sckf->sckr", multiplier_vector, filtered_modes, precision=highest)
    sums = jax.ops.segment_sum(local_terms.reshape(SLAB_TOTAL * COLUMN_TOTAL * KC, RHS), coarse_map.reshape(-1), num_segments=NCOARSE)
    solved = jnp.dot(sums.T.astype(jnp.bfloat16), coarse_inverse, preferred_element_type=jnp.float32)
    picked = solved[:, coarse_map.reshape(-1)].reshape(RHS, SLAB_TOTAL, COLUMN_TOTAL, KC)
    return jnp.einsum("rsck,sckf->scrf", picked, filtered_modes, precision=highest)


def reference(forcing_terms, schur, flexibility, coarse_modes, coarse_map, face_slot_count, coarse_inverse):
    slot_activity = active_mask(face_slot_count)
    filtered_modes = coarse_modes * slot_activity

    def operator(multiplier_vector):
        return gather_owned(subdomain_products(distribute_values(multiplier_vector), flexibility), slot_activity)

    def precondition(multiplier_vector):
        dirichlet_part = 0.25 * gather_owned(subdomain_products(distribute_values(multiplier_vector), schur), slot_activity)
        return dirichlet_part + coarse_term(multiplier_vector, filtered_modes, coarse_map, coarse_inverse)

    def inner_product(first, second):
        return jnp.sum(first * second, axis=(0, 1, 3))

    def per_side(values):
        return values[None, None, :, None]

    residual = slot_activity * forcing_terms
    multipliers = jnp.zeros_like(residual)
    search = precondition(residual)
    product = inner_product(residual, search)
    for iteration in range(ITERS):
        fresh_image = operator(search)
        step_size = product / inner_product(search, fresh_image)
        multipliers = multipliers + per_side(step_size) * search
        residual = residual - per_side(step_size) * fresh_image
        if iteration + 1 < ITERS:
            smoothed = precondition(residual)
            product_next = inner_product(residual, smoothed)
            search = smoothed + per_side(product_next / product) * search
            product = product_next
    return multipliers, residual
```

```python
import functools

import jax
import jax.numpy as jnp
from jax import lax
from jax.experimental import pallas as pl
from jax.experimental.pallas import tpu as pltpu
from jax.sharding import PartitionSpec as P

MESH = pl.DeviceIdType.MESH
F32 = jnp.float32
BF16 = jnp.bfloat16
FD = 256
R = 64
LANES = 128


def split_rows(x):
    hi = x.astype(BF16)
    lo = (x - hi.astype(F32)).astype(BF16)
    return jnp.concatenate([hi, lo], axis=0)


def kernel(
    gx_n, gy_n,
    f_hbm, s_hbm, a_hbm, modes_hbm, map_smem, cnt_smem, cinv_hbm,
    x_out, r_out,
    s_v, a_v, cinv_v, f_v, modes_v,
    stat_v, hf_v, hm_v, hs_v,
    wsend, wrecv, xz_v, xq_v, xu_v, oe_v, cs_v, dsm_v,
    t_v, t16_v, g1_v, g2_v, g3src_v, g3_v, y_v, a8_v,
    lsem, hsend, hrecv, wssem, wrsem, gssem, grsem,
):
    sx = lax.axis_index("gx")
    cy = lax.axis_index("gy")
    rg = R // gy_n
    rows_per_group = LANES // gy_n
    groups = gx_n // rows_per_group
    up_x = lax.rem(sx + 1, gx_n)
    dn_x = lax.rem(sx + gx_n - 1, gx_n)
    up_y = lax.rem(cy + 1, gy_n)
    dn_y = lax.rem(cy + gy_n - 1, gy_n)

    loads = [
        pltpu.make_async_copy(f_hbm.at[0, 0], f_v, lsem.at[0]),
        pltpu.make_async_copy(modes_hbm.at[0, 0], modes_v, lsem.at[1]),
        pltpu.make_async_copy(s_hbm.at[0, 0], s_v, lsem.at[2]),
        pltpu.make_async_copy(cinv_hbm, cinv_v, lsem.at[3]),
        pltpu.make_async_copy(a_hbm.at[0, 0], a_v, lsem.at[4]),
    ]
    for load in loads:
        load.start()

    barrier = pltpu.get_barrier_semaphore()

    def greet_row(i, carry):
        pl.semaphore_signal(barrier, inc=1, device_id=(sx, lax.rem(cy + i, gy_n)), device_id_type=MESH)
        return carry

    def greet_column(i, carry):
        pl.semaphore_signal(barrier, inc=1, device_id=(lax.rem(sx + i, gx_n), cy), device_id_type=MESH)
        return carry

    lax.fori_loop(1, gy_n, greet_row, 0)
    lax.fori_loop(1, gx_n, greet_column, 0)

    lane = lax.broadcasted_iota(jnp.int32, (8, FD), 1)
    sub = lax.broadcasted_iota(jnp.int32, (8, FD), 0)
    map_tile = jnp.zeros((8, FD), jnp.int32)
    for k in range(8):
        map_tile = jnp.where(sub == k, map_smem[0, 0, k], map_tile)
    map_tile = lax.rem(map_tile, LANES).astype(F32)
    live_x = jnp.logical_and(lane < cnt_smem[0, 0, 0], sx < gx_n - 1)
    live_y = jnp.logical_and(lane < cnt_smem[0, 0, 1], cy < gy_n - 1)
    for face, live in ((0, live_x), (1, live_y)):
        stat_v[face, 0:8, :] = map_tile
        stat_v[face, 8:16, :] = jnp.where(live, 1.0, 0.0).astype(F32)

    pl.semaphore_wait(barrier, gy_n + gx_n - 2)

    halo = []
    for face, target in ((0, (up_x, cy)), (1, (sx, up_y))):
        cols = pl.ds(face * FD, FD)
        for n, (src, dst) in enumerate((
            (stat_v.at[face], hs_v.at[face]),
            (modes_hbm.at[0, 0, :, cols], hm_v.at[face]),
            (f_hbm.at[0, 0, :, cols], hf_v.at[face]),
        )):
            copy = pltpu.make_async_remote_copy(
                src_ref=src, dst_ref=dst, send_sem=hsend.at[face, n], recv_sem=hrecv.at[face, n],
                device_id=target, device_id_type=MESH,
            )
            copy.start()
            halo.append(copy)

    sub_l = lax.broadcasted_iota(jnp.int32, (LANES, FD), 0).astype(F32)

    def basis_block(block, maps, modes):
        total = jnp.zeros((LANES, FD), F32)
        for k in range(8):
            total = total + jnp.where(sub_l == maps[k : k + 1, :], modes[k : k + 1, :], 0.0)
        hi = total.astype(BF16)
        cols = slice(block * FD, (block + 1) * FD)
        oe_v[0:LANES, cols] = hi
        oe_v[LANES:, cols] = (total - hi.astype(F32)).astype(BF16)

    def own_live(face):
        return stat_v[face, 8:9, :]

    def all_live(block):
        face = block // 2
        if block % 2:
            return stat_v[face, 8:9, :]
        inside = (sx > 0) if face == 0 else (cy > 0)
        return jnp.where(inside, hs_v[face, 8:9, :], 0.0)

    def scatter_rows(n, tile):
        t_v[...] = tile
        for i in range(gy_n):
            t16_v[n, i] = t_v[i * rg : (i + 1) * rg, :]
        g1_v[n, cy] = t16_v[n, cy]

        def send(i, carry):
            to = lax.rem(cy + i, gy_n)
            pltpu.make_async_remote_copy(
                src_ref=t16_v.at[n, to], dst_ref=g1_v.at[n, cy], send_sem=gssem.at[n, 0], recv_sem=grsem.at[n, 0],
                device_id=(sx, to), device_id_type=MESH,
            ).start()
            return carry

        lax.fori_loop(1, gy_n, send, 0)

    def wait_all(ref, n, phase, recv):
        copy = pltpu.make_async_remote_copy(
            src_ref=ref, dst_ref=ref, send_sem=gssem.at[n, phase], recv_sem=grsem.at[n, phase],
            device_id=(sx, up_y), device_id_type=MESH,
        )
        if recv:
            copy.wait_recv()
        else:
            copy.wait_send()

    def gather_columns(n):
        wait_all(g1_v.at[n, pl.ds(0, gy_n - 1)], n, 0, True)
        total = g1_v[n, 0]
        for i in range(1, gy_n):
            total = total + g1_v[n, i]
        g2_v[n, sx] = total

        def send(i, carry):
            pltpu.make_async_remote_copy(
                src_ref=g2_v.at[n, sx], dst_ref=g2_v.at[n, sx], send_sem=gssem.at[n, 1], recv_sem=grsem.at[n, 1],
                device_id=(lax.rem(sx + i, gx_n), cy), device_id_type=MESH,
            ).start()
            return carry

        lax.fori_loop(1, gx_n, send, 0)

    def wait_columns(n):
        wait_all(g2_v.at[n, pl.ds(0, gx_n - 1)], n, 1, True)

    def give_rows(n, tile):
        g3_v[n, cy] = tile

        def send(i, carry):
            pltpu.make_async_remote_copy(
                src_ref=g3_v.at[n, cy], dst_ref=g3_v.at[n, cy], send_sem=gssem.at[n, 2], recv_sem=grsem.at[n, 2],
                device_id=(sx, lax.rem(cy + i, gy_n)), device_id_type=MESH,
            ).start()
            return carry

        lax.fori_loop(1, gy_n, send, 0)

    def take_rows(n):
        wait_all(g3_v.at[n, pl.ds(0, gy_n - 1)], n, 2, True)
        for i in range(gy_n):
            y_v[i * rg : (i + 1) * rg, :] = g3_v[n, i]
        return y_v[...]

    lane_g = lax.broadcasted_iota(jnp.int32, (rg, LANES), 1)

    def solve(n):
        wait_columns(n)
        for g in range(groups):
            base = g * rows_per_group
            last = base + rows_per_group - 1
            total = jnp.where(lane_g < LANES - gy_n, g2_v[n, base], 0.0)
            total = total + jnp.where(lane_g >= gy_n, g2_v[n, last], 0.0)
            for z in range(base + 1, last):
                total = total + g2_v[n, z]
            if g > 0:
                total = total + jnp.where(lane_g < gy_n, g2_v[n, base - 1], 0.0)
            if g < groups - 1:
                total = total + jnp.where(lane_g >= LANES - gy_n, g2_v[n, last + 1], 0.0)
            hi = total.astype(BF16).astype(F32)
            cols = slice(g * LANES, (g + 1) * LANES)
            a8_v[0:rg, cols] = hi
            a8_v[rg : 2 * rg, cols] = total - hi
        res = jnp.dot(a8_v[...].astype(BF16), cs_v[...], preferred_element_type=F32)
        g3src_v[...] = res
        give_rows(n, g3src_v[0:rg, :] + g3src_v[rg : 2 * rg, :])

    def restrict(xx, basis):
        t4 = lax.dot_general(xx, basis, (((1,), (1,)), ((), ())), preferred_element_type=F32)
        return (t4[:R, :LANES] + t4[R:, LANES:]) + (t4[R:, :LANES] + t4[:R, LANES:])

    def prolong(n):
        y = take_rows(n)
        hi = y.astype(BF16)
        lo = (y - hi.astype(F32)).astype(BF16)
        both = jnp.concatenate([jnp.concatenate([hi, hi], axis=1), jnp.concatenate([lo, lo], axis=1)], axis=0)
        return both

    def prolong_block(both, block):
        out = jnp.dot(both, oe_v[:, block * FD : (block + 1) * FD], preferred_element_type=F32)
        return out[:R] + out[R:]

    targets = {0: (dn_x, cy), 1: (up_x, cy), 2: (sx, dn_y), 3: (sx, up_y)}

    def face_copy(op, block):
        return pltpu.make_async_remote_copy(
            src_ref=wsend.at[op, block], dst_ref=wrecv.at[op, block ^ 1],
            send_sem=wssem.at[op, block], recv_sem=wrsem.at[op, block ^ 1],
            device_id=targets[block], device_id_type=MESH,
        )

    def apply(op, xx, matrix, order=(0, 1, 2, 3), send=(0, 1, 2, 3)):
        for block in order:
            out = jnp.dot(xx, matrix[:, block * FD : (block + 1) * FD], preferred_element_type=F32)
            wsend[op, block] = out[:R] + out[R:]
            if block in send:
                face_copy(op, block).start()

    def collected(op, block):
        return jnp.where(all_live(block) > 0.5, wsend[op, block] - wrecv[op, block], 0.0)

    def wait_faces(op, blocks=(0, 1, 2, 3)):
        for block in blocks:
            face_copy(op, block ^ 1).wait_recv()

    loads[0].wait()
    loads[1].wait()
    r_own = []
    for face in range(2):
        cols = slice(face * FD, (face + 1) * FD)
        live = own_live(face)
        r_own.append(jnp.where(live > 0.5, f_v[:, cols], 0.0))
        basis_block(2 * face + 1, stat_v[face, 0:8, :], modes_v[:, cols] * live)
    basis_own = jnp.concatenate([oe_v[:, FD : 2 * FD], oe_v[:, 3 * FD :]], axis=1)
    scatter_rows(0, restrict(split_rows(jnp.concatenate(r_own, axis=1)), basis_own))

    halo[0].wait_recv()
    halo[1].wait_recv()
    halo[3].wait_recv()
    halo[4].wait_recv()
    for face in range(2):
        basis_block(2 * face, hs_v[face, 0:8, :], -(hm_v[face] * all_live(2 * face)))
    halo[2].wait_recv()
    halo[5].wait_recv()
    x0 = jnp.concatenate(
        [
            -jnp.where(all_live(0) > 0.5, hf_v[0], 0.0),
            r_own[0],
            -jnp.where(all_live(2) > 0.5, hf_v[1], 0.0),
            r_own[1],
        ],
        axis=1,
    )
    loads[2].wait()
    apply(0, split_rows(x0), s_v)
    gather_columns(0)

    loads[3].wait()
    lane_c = lax.broadcasted_iota(jnp.int32, (1, LANES), 1)
    cs = jnp.zeros((groups * LANES, LANES), BF16)
    for g in range(groups):
        row = g * rows_per_group + lane_c // gy_n
        near = jnp.logical_and(row >= sx - 1, row <= sx + 1)
        near = jnp.where(near, 1.0, 0.0).astype(BF16)
        cs = cs + cinv_v[:, g * LANES : (g + 1) * LANES] * near
    cs_v[...] = cs

    solve(0)
    both = prolong(0)
    coarse = [prolong_block(both, block) for block in range(4)]
    wait_faces(0)
    for block in range(4):
        xz_v[:, block * FD : (block + 1) * FD] = 0.25 * collected(0, block) + coarse[block]

    loads[4].wait()
    apply(1, split_rows(xz_v[...]), a_v)
    w0 = jnp.concatenate([wsend[1, block] for block in range(4)], axis=1)
    scatter_rows(1, restrict(split_rows(w0), oe_v[...]))

    def owned_dot(a, b):
        return jnp.sum(a[0] * b[0], axis=1, keepdims=True) + jnp.sum(a[1] * b[1], axis=1, keepdims=True)

    def owned(ref):
        return ref[:, FD : 2 * FD], ref[:, 3 * FD :]

    gamma0 = owned_dot(r_own, owned(xz_v))
    delta0 = jnp.sum(xz_v[...] * w0, axis=1, keepdims=True)

    wait_faces(1)
    for block in range(4):
        xq_v[:, block * FD : (block + 1) * FD] = collected(1, block)
    apply(2, split_rows(xq_v[...]), s_v)
    gather_columns(1)
    solve(1)
    both = prolong(1)
    coarse = [prolong_block(both, block) for block in range(4)]
    wait_faces(2)
    for block in range(4):
        xu_v[:, block * FD : (block + 1) * FD] = 0.25 * collected(2, block) + coarse[block]

    apply(3, split_rows(xu_v[...]), a_v, order=(0, 2, 1, 3), send=(0, 2))
    wu = jnp.concatenate([wsend[3, block] for block in range(4)], axis=1)
    sums = (
        gamma0,
        delta0,
        owned_dot(r_own, owned(xu_v)),
        owned_dot(owned(xq_v), owned(xu_v)),
        jnp.sum(xz_v[...] * wu + xu_v[...] * w0, axis=1, keepdims=True),
        jnp.sum(xu_v[...] * wu, axis=1, keepdims=True),
    )
    lane_r = lax.broadcasted_iota(jnp.int32, (R, LANES), 1)
    tile = jnp.zeros((R, LANES), F32)
    for j, value in enumerate(sums):
        tile = jnp.where(lane_r == j, value, tile)
    scatter_rows(2, tile)
    gather_columns(2)
    wait_columns(2)
    total = g2_v[2, 0]
    for i in range(1, gx_n):
        total = total + g2_v[2, i]
    give_rows(2, total)
    wait_faces(3, (1, 3))
    scalars = take_rows(2)
    g0, d0, ru, qu, cross, uu = (scalars[:, j : j + 1] for j in range(6))
    alpha0 = g0 / d0
    g1 = alpha0 * (alpha0 * qu - ru)
    beta1 = 1.0 + g1 / g0
    d1 = beta1 * (beta1 * d0 - alpha0 * cross) + alpha0 * alpha0 * uu
    alpha1 = g1 / d1
    first = alpha0 + alpha1 * beta1
    second = alpha0 * alpha1
    for face in range(2):
        block = 2 * face + 1
        cols = slice(face * FD, (face + 1) * FD)
        own = slice(block * FD, (block + 1) * FD)
        x_out[0, 0, :, cols] = first * xz_v[:, own] - second * xu_v[:, own]
        r_out[0, 0, :, cols] = r_own[face] - first * xq_v[:, own] + second * collected(3, block)

    for copy in halo:
        copy.wait_send()
    for op in range(4):
        for block in (0, 1, 2, 3) if op < 3 else (0, 2):
            face_copy(op, block).wait_send()
    for n in range(3):
        wait_all(t16_v.at[n, pl.ds(0, gy_n - 1)], n, 0, False)
        wait_all(g2_v.at[n, pl.ds(0, gx_n - 1)], n, 1, False)
        wait_all(g3_v.at[n, pl.ds(0, gy_n - 1)], n, 2, False)


def on_device(mesh_shape, forcing_terms, schur, flexibility, coarse_modes, coarse_map, face_slot_count, coarse_inverse):
    gx_n, gy_n = mesh_shape
    rg = R // gy_n
    nb = 4 * FD
    hbm = pl.BlockSpec(memory_space=pl.ANY)
    smem = pl.BlockSpec(memory_space=pltpu.SMEM)
    vmem = pl.BlockSpec(memory_space=pltpu.VMEM)
    out = jax.ShapeDtypeStruct(forcing_terms.shape, F32)
    return pl.pallas_call(
        functools.partial(kernel, gx_n, gy_n),
        out_shape=(out, out),
        in_specs=[hbm, hbm, hbm, hbm, smem, smem, hbm],
        out_specs=(vmem, vmem),
        scratch_shapes=[
            pltpu.VMEM((nb, nb), BF16),
            pltpu.VMEM((nb, nb), BF16),
            pltpu.VMEM(coarse_inverse.shape, BF16),
            pltpu.VMEM((R, 2 * FD), F32),
            pltpu.VMEM((8, 2 * FD), F32),
            pltpu.VMEM((2, 16, FD), F32),
            pltpu.VMEM((2, R, FD), F32),
            pltpu.VMEM((2, 8, FD), F32),
            pltpu.VMEM((2, 16, FD), F32),
            pltpu.VMEM((4, 4, R, FD), F32),
            pltpu.VMEM((4, 4, R, FD), F32),
            pltpu.VMEM((R, nb), F32),
            pltpu.VMEM((R, nb), F32),
            pltpu.VMEM((R, nb), F32),
            pltpu.VMEM((2 * LANES, nb), BF16),
            pltpu.VMEM((gx_n * gy_n, LANES), BF16),
            pltpu.VMEM((8, LANES), F32),
            pltpu.VMEM((R, LANES), F32),
            pltpu.VMEM((3, gy_n, rg, LANES), F32),
            pltpu.VMEM((3, gy_n, rg, LANES), F32),
            pltpu.VMEM((3, gx_n, rg, LANES), F32),
            pltpu.VMEM((2 * rg, LANES), F32),
            pltpu.VMEM((3, gy_n, rg, LANES), F32),
            pltpu.VMEM((R, LANES), F32),
            pltpu.VMEM((2 * rg, gx_n * gy_n), F32),
            pltpu.SemaphoreType.DMA((5,)),
            pltpu.SemaphoreType.DMA((2, 3)),
            pltpu.SemaphoreType.DMA((2, 3)),
            pltpu.SemaphoreType.DMA((4, 4)),
            pltpu.SemaphoreType.DMA((4, 4)),
            pltpu.SemaphoreType.DMA((3, 3)),
            pltpu.SemaphoreType.DMA((3, 3)),
        ],
        compiler_params=pltpu.CompilerParams(
            collective_id=0, has_side_effects=True, vmem_limit_bytes=56 * 1024 * 1024
        ),
    )(forcing_terms, schur, flexibility, coarse_modes, coarse_map, face_slot_count, coarse_inverse)


def solution(mesh):
    shape = (mesh.shape["gx"], mesh.shape["gy"])
    return jax.shard_map(
        functools.partial(on_device, shape),
        mesh=mesh,
        in_specs=(
            P("gx", "gy", None, None),
            P("gx", "gy", None, None),
            P("gx", "gy", None, None),
            P("gx", "gy", None, None),
            P("gx", "gy", None),
            P("gx", "gy", None),
            P(),
        ),
        out_specs=(P("gx", "gy", None, None), P("gx", "gy", None, None)),
        check_vma=False,
    )
```

```python
import functools

import jax
import jax.numpy as jnp
from jax import lax
from jax.experimental import pallas as pl
from jax.experimental.pallas import tpu as pltpu
from jax.sharding import PartitionSpec as P

MESH = pl.DeviceIdType.MESH
F32 = jnp.float32
BF16 = jnp.bfloat16
FD = 256
R = 64
LANES = 128
OFFSETS = ((0, 0), (0, 1), (1, 0), (1, 1), (-1, 0), (-1, 1), (0, -1), (1, -1))


def split_rows(x):
    hi = x.astype(BF16)
    lo = (x - hi.astype(F32)).astype(BF16)
    return jnp.concatenate([hi, lo], axis=0)


def corner_shift(j, columns):
    shift = jnp.zeros_like(j)
    for n, (a, b) in enumerate(OFFSETS):
        shift = jnp.where(j == n, a * columns + b, shift)
    return shift


def kernel(
    gx_n, gy_n,
    f_hbm, s_hbm, a_hbm, modes_hbm, map_smem, cnt_smem, cinv_hbm,
    x_out, r_out,
    s_v, a_v, cinv_v, f_v, modes_v,
    stat_v, hf_v, hm_v, hs_v,
    wsend, wrecv, xz_v, xq_v, xu_v, oe_v, oe2_v, q_v,
    g1_v, part_v, g2_v,
    lsem, hsend, hrecv, wssem, wrsem, gssem, grsem,
):
    sx = lax.axis_index("gx")
    cy = lax.axis_index("gy")
    corners = gx_n * gy_n
    up_x = lax.rem(sx + 1, gx_n)
    dn_x = lax.rem(sx + gx_n - 1, gx_n)
    up_y = lax.rem(cy + 1, gy_n)
    dn_y = lax.rem(cy + gy_n - 1, gy_n)

    loads = [
        pltpu.make_async_copy(f_hbm.at[0, 0], f_v, lsem.at[0]),
        pltpu.make_async_copy(modes_hbm.at[0, 0], modes_v, lsem.at[1]),
        pltpu.make_async_copy(cinv_hbm, cinv_v, lsem.at[2]),
        pltpu.make_async_copy(s_hbm.at[0, 0], s_v, lsem.at[3]),
        pltpu.make_async_copy(a_hbm.at[0, 0], a_v, lsem.at[4]),
    ]
    for load in loads:
        load.start()

    def each_row(send):
        half = gy_n // 2
        send(lax.rem(cy + half, gy_n))

        def pair(i, carry):
            send(lax.rem(cy + half + i, gy_n))
            send(lax.rem(cy + half - i, gy_n))
            return carry

        lax.fori_loop(1, half, pair, 0)

    def each_column(send):
        x_n, z_n = 4, gx_n // 4
        half = z_n // 2
        x_at, z_at = sx // z_n, lax.rem(sx, z_n)

        def level(dz, shifts=(2, 1, 3, 0)):
            z_to = lax.rem(z_at + dz, z_n)
            for dx in shifts:
                send(lax.rem(x_at + dx, x_n) * z_n + z_to)

        level(half)

        def pair(i, carry):
            level(half + i)
            level(half - i)
            return carry

        lax.fori_loop(1, half, pair, 0)
        level(0, (2, 1, 3))

    barrier = pltpu.get_barrier_semaphore()

    def greet(target):
        pl.semaphore_signal(barrier, inc=1, device_id=target, device_id_type=MESH)

    each_column(lambda to: greet((to, cy)))
    each_row(lambda to: greet((sx, to)))

    lane = lax.broadcasted_iota(jnp.int32, (8, FD), 1)
    sub = lax.broadcasted_iota(jnp.int32, (8, FD), 0)
    map_tile = jnp.zeros((8, FD), jnp.int32)
    for k in range(8):
        map_tile = jnp.where(sub == k, map_smem[0, 0, k], map_tile)
    map_tile = map_tile.astype(F32)
    live_x = jnp.logical_and(lane < cnt_smem[0, 0, 0], sx < gx_n - 1)
    live_y = jnp.logical_and(lane < cnt_smem[0, 0, 1], cy < gy_n - 1)
    for face, live in ((0, live_x), (1, live_y)):
        stat_v[face, 0:8, :] = map_tile
        stat_v[face, 8:16, :] = jnp.where(live, 1.0, 0.0).astype(F32)

    corner = (sx * gy_n + cy + corner_shift(sub, gy_n)).astype(F32)

    def basis_block(block, maps, modes):
        total = jnp.zeros((8, FD), F32)
        for k in range(8):
            total = total + jnp.where(corner == maps[k : k + 1, :], modes[k : k + 1, :], 0.0)
        hi = total.astype(BF16).astype(F32)
        lo = total - hi
        cols = slice(block * FD, (block + 1) * FD)
        oe_v[:, cols] = jnp.concatenate([hi, lo], axis=0).astype(BF16)
        oe2_v[:, cols] = jnp.concatenate([hi, hi, lo, lo], axis=0).astype(BF16)

    def own_live(face):
        return stat_v[face, 8:9, :]

    def all_live(block):
        face = block // 2
        if block % 2:
            return stat_v[face, 8:9, :]
        inside = (sx > 0) if face == 0 else (cy > 0)
        return jnp.where(inside, hs_v[face, 8:9, :], 0.0)

    def row_send(n, tile):
        g1_v[n, cy] = tile

        def send(to):
            pltpu.make_async_remote_copy(
                src_ref=g1_v.at[n, cy], dst_ref=g1_v.at[n, cy], send_sem=gssem.at[n, 0], recv_sem=grsem.at[n, 0],
                device_id=(sx, to), device_id_type=MESH,
            ).start()

        each_row(send)

    def column_send(n, source):
        def send(to):
            pltpu.make_async_remote_copy(
                src_ref=source(to), dst_ref=g2_v.at[n, sx], send_sem=gssem.at[n, 1], recv_sem=grsem.at[n, 1],
                device_id=(to, cy), device_id_type=MESH,
            ).start()

        each_column(send)

    def wait_all(ref, n, phase, recv):
        copy = pltpu.make_async_remote_copy(
            src_ref=ref, dst_ref=ref, send_sem=gssem.at[n, phase], recv_sem=grsem.at[n, phase],
            device_id=(sx, up_y), device_id_type=MESH,
        )
        if recv:
            copy.wait_recv()
        else:
            copy.wait_send()

    def wait_row(n):
        wait_all(g1_v.at[n, pl.ds(0, gy_n - 1)], n, 0, True)

    def wait_column(n):
        wait_all(g2_v.at[n, pl.ds(0, gx_n - 1)], n, 1, True)

    def tree(values):
        while len(values) > 1:
            values = [a + b for a, b in zip(values[::2], values[1::2])]
        return values[0]

    def restrict(xx, basis):
        t = lax.dot_general(basis, xx, (((1,), (1,)), ((), ())), preferred_element_type=F32)
        t = t[0:8] + t[8:16]
        return t + pltpu.roll(t, R, 1)

    lane_g = lax.broadcasted_iota(jnp.int32, (LANES, LANES), 1)

    def solve(n):
        wait_row(n)
        sums = g1_v[n].reshape(LANES, LANES)
        hi = sums.astype(BF16).astype(F32)
        terms = jnp.where(lane_g < R, hi, sums - hi).astype(BF16)
        part = jnp.dot(q_v[...], terms, preferred_element_type=F32)
        part_v[n] = part.reshape(gx_n, 8, LANES)
        g2_v[n, sx] = part_v[n, sx]
        column_send(n, lambda to: part_v.at[n, to])

    def prolong(n):
        wait_column(n)
        y = tree([g2_v[n, i] for i in range(gx_n)])
        y = y + pltpu.roll(y, R, 1)
        hi = y.astype(BF16).astype(F32)
        lo = y - hi
        terms = jnp.concatenate([hi, lo, hi, lo], axis=0)
        return jnp.transpose(terms)[:R].astype(BF16)

    def prolong_block(terms, block):
        return jnp.dot(terms, oe2_v[:, block * FD : (block + 1) * FD], preferred_element_type=F32)

    targets = {0: (dn_x, cy), 1: (up_x, cy), 2: (sx, dn_y), 3: (sx, up_y)}

    def face_copy(op, block):
        return pltpu.make_async_remote_copy(
            src_ref=wsend.at[op, block], dst_ref=wrecv.at[op, block ^ 1],
            send_sem=wssem.at[op, block], recv_sem=wrsem.at[op, block ^ 1],
            device_id=targets[block], device_id_type=MESH,
        )

    def apply(op, xx, matrix, order=(0, 1, 2, 3), send=(0, 1, 2, 3)):
        for block in order:
            out = jnp.dot(xx, matrix[:, block * FD : (block + 1) * FD], preferred_element_type=F32)
            wsend[op, block] = out[:R] + out[R:]
            if block in send:
                face_copy(op, block).start()

    def collected(op, block):
        return jnp.where(all_live(block) > 0.5, wsend[op, block] - wrecv[op, block], 0.0)

    def wait_faces(op, blocks=(0, 1, 2, 3)):
        for block in blocks:
            face_copy(op, block ^ 1).wait_recv()

    loads[0].wait()
    loads[1].wait()
    r_own = []
    for face in range(2):
        cols = slice(face * FD, (face + 1) * FD)
        live = own_live(face)
        r_own.append(jnp.where(live > 0.5, f_v[:, cols], 0.0))
        basis_block(2 * face + 1, stat_v[face, 0:8, :], modes_v[:, cols] * live)
    basis_own = jnp.concatenate([oe_v[:, FD : 2 * FD], oe_v[:, 3 * FD :]], axis=1)
    first_sums = restrict(split_rows(jnp.concatenate(r_own, axis=1)), basis_own)

    pl.semaphore_wait(barrier, gy_n + gx_n - 2)

    row_send(0, first_sums)
    halo = []
    for face, target in ((0, (up_x, cy)), (1, (sx, up_y))):
        cols = pl.ds(face * FD, FD)
        for n, (src, dst) in enumerate((
            (stat_v.at[face], hs_v.at[face]),
            (modes_v.at[:, cols], hm_v.at[face]),
            (f_v.at[:, cols], hf_v.at[face]),
        )):
            copy = pltpu.make_async_remote_copy(
                src_ref=src, dst_ref=dst, send_sem=hsend.at[face, n], recv_sem=hrecv.at[face, n],
                device_id=target, device_id_type=MESH,
            )
            copy.start()
            halo.append(copy)

    loads[2].wait()
    row_q = lax.broadcasted_iota(jnp.int32, (8 * gx_n, LANES), 0)
    lane_q = lax.broadcasted_iota(jnp.int32, (8 * gx_n, LANES), 1)
    at = (row_q // 8) * gy_n + cy + corner_shift(lax.rem(row_q, 8), gy_n) - lane_q
    pick = [jnp.where(at == g * LANES, 1.0, 0.0).astype(BF16) for g in range(corners // LANES)]
    to_column = lax.dot_general(
        jnp.concatenate(pick, axis=1), cinv_v[...], (((1,), (1,)), ((), ())), preferred_element_type=F32
    ).astype(BF16)
    row_p = lax.broadcasted_iota(jnp.int32, (8 * gy_n, LANES), 0)
    lane_p = lax.broadcasted_iota(jnp.int32, (8 * gy_n, LANES), 1)
    at = sx * gy_n + row_p // 8 + corner_shift(lax.rem(row_p, 8), gy_n) - lane_p
    pick = [jnp.where(at == g * LANES, 1.0, 0.0).astype(BF16) for g in range(corners // LANES)]
    q_v[...] = lax.dot_general(
        to_column, jnp.concatenate(pick, axis=1), (((1,), (1,)), ((), ())), preferred_element_type=F32
    ).astype(BF16)

    halo[2].wait_recv()
    halo[5].wait_recv()
    halo[0].wait_recv()
    halo[3].wait_recv()
    x0 = jnp.concatenate(
        [
            -jnp.where(all_live(0) > 0.5, hf_v[0], 0.0),
            r_own[0],
            -jnp.where(all_live(2) > 0.5, hf_v[1], 0.0),
            r_own[1],
        ],
        axis=1,
    )
    loads[3].wait()
    apply(0, split_rows(x0), s_v)
    solve(0)

    halo[1].wait_recv()
    halo[4].wait_recv()
    for face in range(2):
        basis_block(2 * face, hs_v[face, 0:8, :], -(hm_v[face] * all_live(2 * face)))

    wait_faces(0)
    for block in range(4):
        xz_v[:, block * FD : (block + 1) * FD] = 0.25 * collected(0, block)
    loads[4].wait()
    terms = prolong(0)
    for block in range(4):
        xz_v[:, block * FD : (block + 1) * FD] += prolong_block(terms, block)

    apply(1, split_rows(xz_v[...]), a_v)
    w0 = jnp.concatenate([wsend[1, block] for block in range(4)], axis=1)
    row_send(1, restrict(split_rows(w0), oe_v[...]))

    def owned_dot(a, b):
        return jnp.sum(a[0] * b[0], axis=1, keepdims=True) + jnp.sum(a[1] * b[1], axis=1, keepdims=True)

    def owned(ref):
        return ref[:, FD : 2 * FD], ref[:, 3 * FD :]

    gamma0 = owned_dot(r_own, owned(xz_v))
    delta0 = jnp.sum(xz_v[...] * w0, axis=1, keepdims=True)

    wait_faces(1)
    for block in range(4):
        xq_v[:, block * FD : (block + 1) * FD] = collected(1, block)
    apply(2, split_rows(xq_v[...]), s_v)
    solve(1)
    wait_faces(2)
    for block in range(4):
        xu_v[:, block * FD : (block + 1) * FD] = 0.25 * collected(2, block)
    terms = prolong(1)
    for block in range(4):
        xu_v[:, block * FD : (block + 1) * FD] += prolong_block(terms, block)

    apply(3, split_rows(xu_v[...]), a_v, order=(0, 2, 1, 3), send=(0, 2))
    wu = jnp.concatenate([wsend[3, block] for block in range(4)], axis=1)
    sums = (
        gamma0,
        delta0,
        owned_dot(r_own, owned(xu_v)),
        owned_dot(owned(xq_v), owned(xu_v)),
        jnp.sum(xz_v[...] * wu + xu_v[...] * w0, axis=1, keepdims=True),
        jnp.sum(xu_v[...] * wu, axis=1, keepdims=True),
    )
    lane_r = lax.broadcasted_iota(jnp.int32, (LANES, LANES), 1)
    tile = jnp.zeros((LANES, LANES), F32)
    for j, value in enumerate(sums):
        tile = jnp.where(lane_r == j, jnp.concatenate([value, value], axis=0), tile)
    row_send(2, jnp.transpose(tile)[0:8])
    wait_row(2)
    g2_v[2, sx] = tree([g1_v[2, i] for i in range(gy_n)])
    column_send(2, lambda to: g2_v.at[2, sx])
    wait_faces(3, (1, 3))
    wait_column(2)
    scalars = tree([g2_v[2, i] for i in range(gx_n)])
    g0, d0, ru, qu, cross, uu = (scalars[j : j + 1] for j in range(6))
    alpha0 = g0 / d0
    g1 = alpha0 * (alpha0 * qu - ru)
    beta1 = 1.0 + g1 / g0
    d1 = beta1 * (beta1 * d0 - alpha0 * cross) + alpha0 * alpha0 * uu
    alpha1 = g1 / d1
    sub_s = lax.broadcasted_iota(jnp.int32, (8, LANES), 0)
    steps = jnp.where(sub_s == 0, alpha0 + alpha1 * beta1, alpha0 * alpha1)
    steps = jnp.transpose(steps)[:R]
    first, second = steps[:, 0:1], steps[:, 1:2]
    for face in range(2):
        block = 2 * face + 1
        cols = slice(face * FD, (face + 1) * FD)
        own = slice(block * FD, (block + 1) * FD)
        x_out[0, 0, :, cols] = first * xz_v[:, own] - second * xu_v[:, own]
        r_out[0, 0, :, cols] = r_own[face] - first * xq_v[:, own] + second * collected(3, block)

    for copy in halo:
        copy.wait_send()
    for op in range(4):
        for block in (0, 1, 2, 3) if op < 3 else (0, 2):
            face_copy(op, block).wait_send()
    for n in range(3):
        wait_all(g1_v.at[n, pl.ds(0, gy_n - 1)], n, 0, False)
        wait_all(g2_v.at[n, pl.ds(0, gx_n - 1)], n, 1, False)


def on_device(mesh_shape, forcing_terms, schur, flexibility, coarse_modes, coarse_map, face_slot_count, coarse_inverse):
    gx_n, gy_n = mesh_shape
    nb = 4 * FD
    hbm = pl.BlockSpec(memory_space=pl.ANY)
    smem = pl.BlockSpec(memory_space=pltpu.SMEM)
    vmem = pl.BlockSpec(memory_space=pltpu.VMEM)
    out = jax.ShapeDtypeStruct(forcing_terms.shape, F32)
    return pl.pallas_call(
        functools.partial(kernel, gx_n, gy_n),
        out_shape=(out, out),
        in_specs=[hbm, hbm, hbm, hbm, smem, smem, hbm],
        out_specs=(vmem, vmem),
        scratch_shapes=[
            pltpu.VMEM((nb, nb), BF16),
            pltpu.VMEM((nb, nb), BF16),
            pltpu.VMEM(coarse_inverse.shape, BF16),
            pltpu.VMEM((R, 2 * FD), F32),
            pltpu.VMEM((8, 2 * FD), F32),
            pltpu.VMEM((2, 16, FD), F32),
            pltpu.VMEM((2, R, FD), F32),
            pltpu.VMEM((2, 8, FD), F32),
            pltpu.VMEM((2, 16, FD), F32),
            pltpu.VMEM((4, 4, R, FD), F32),
            pltpu.VMEM((4, 4, R, FD), F32),
            pltpu.VMEM((R, nb), F32),
            pltpu.VMEM((R, nb), F32),
            pltpu.VMEM((R, nb), F32),
            pltpu.VMEM((16, nb), BF16),
            pltpu.VMEM((32, nb), BF16),
            pltpu.VMEM((8 * gx_n, 8 * gy_n), BF16),
            pltpu.VMEM((3, gy_n, 8, LANES), F32),
            pltpu.VMEM((2, gx_n, 8, LANES), F32),
            pltpu.VMEM((3, gx_n, 8, LANES), F32),
            pltpu.SemaphoreType.DMA((5,)),
            pltpu.SemaphoreType.DMA((2, 3)),
            pltpu.SemaphoreType.DMA((2, 3)),
            pltpu.SemaphoreType.DMA((4, 4)),
            pltpu.SemaphoreType.DMA((4, 4)),
            pltpu.SemaphoreType.DMA((3, 2)),
            pltpu.SemaphoreType.DMA((3, 2)),
        ],
        compiler_params=pltpu.CompilerParams(
            collective_id=0, has_side_effects=True, vmem_limit_bytes=56 * 1024 * 1024
        ),
    )(forcing_terms, schur, flexibility, coarse_modes, coarse_map, face_slot_count, coarse_inverse)


def solution(mesh):
    shape = (mesh.shape["gx"], mesh.shape["gy"])
    return jax.shard_map(
        functools.partial(on_device, shape),
        mesh=mesh,
        in_specs=(
            P("gx", "gy", None, None),
            P("gx", "gy", None, None),
            P("gx", "gy", None, None),
            P("gx", "gy", None, None),
            P("gx", "gy", None),
            P("gx", "gy", None),
            P(),
        ),
        out_specs=(P("gx", "gy", None, None), P("gx", "gy", None, None)),
        check_vma=False,
    )
```

```python
import functools

import jax
import jax.numpy as jnp
from jax import lax
from jax.experimental import pallas as pl
from jax.experimental.pallas import tpu as pltpu
from jax.sharding import PartitionSpec as P

MESH = pl.DeviceIdType.MESH
F32 = jnp.float32
BF16 = jnp.bfloat16
FD = 256
R = 64
LANES = 128
OFFSETS = ((0, 0), (0, 1), (1, 0), (1, 1), (-1, 0), (-1, 1), (0, -1), (1, -1))


def split_rows(x):
    hi = x.astype(BF16)
    lo = (x - hi.astype(F32)).astype(BF16)
    return jnp.concatenate([hi, lo], axis=0)


def corner_shift(j, columns):
    shift = jnp.zeros_like(j)
    for n, (a, b) in enumerate(OFFSETS):
        shift = jnp.where(j == n, a * columns + b, shift)
    return shift


def kernel(
    gx_n, gy_n,
    f_hbm, s_hbm, a_hbm, modes_hbm, map_smem, cnt_smem, cinv_hbm,
    out_v,
    s_v, a_v, cinv_v, f_v, modes_v,
    stat_v, hf_v, hm_v, hs_v,
    wsend, wrecv, xz_v, xq_v, xu_v, oe_v, oe2_v, oef_v, oef2_v, gram_v, q_v,
    g1_v, part_v, g2_v,
    lsem, hsend, hrecv, wssem, wrsem, gssem, grsem,
):
    sx = lax.axis_index("gx")
    cy = lax.axis_index("gy")
    corners = gx_n * gy_n
    up_x = lax.rem(sx + 1, gx_n)
    dn_x = lax.rem(sx + gx_n - 1, gx_n)
    up_y = lax.rem(cy + 1, gy_n)
    dn_y = lax.rem(cy + gy_n - 1, gy_n)

    loads = [
        pltpu.make_async_copy(f_hbm.at[0, 0], f_v, lsem.at[0]),
        pltpu.make_async_copy(modes_hbm.at[0, 0], modes_v, lsem.at[1]),
        pltpu.make_async_copy(cinv_hbm, cinv_v, lsem.at[2]),
        pltpu.make_async_copy(s_hbm.at[0, 0], s_v, lsem.at[3]),
        pltpu.make_async_copy(a_hbm.at[0, 0], a_v, lsem.at[4]),
    ]
    for load in loads:
        load.start()

    def each_row(send):
        half = gy_n // 2
        send(lax.rem(cy + half, gy_n))

        def pair(i, carry):
            send(lax.rem(cy + half + i, gy_n))
            send(lax.rem(cy + half - i, gy_n))
            return carry

        lax.fori_loop(1, half, pair, 0)

    def each_column(send):
        x_n, z_n = 4, gx_n // 4
        half = z_n // 2
        x_at, z_at = sx // z_n, lax.rem(sx, z_n)

        def level(dz, shifts=(2, 1, 3, 0)):
            z_to = lax.rem(z_at + dz, z_n)
            for dx in shifts:
                send(lax.rem(x_at + dx, x_n) * z_n + z_to)

        level(half)

        def pair(i, carry):
            level(half + i)
            level(half - i)
            return carry

        lax.fori_loop(1, half, pair, 0)
        level(0, (2, 1, 3))

    barrier = pltpu.get_barrier_semaphore()

    def greet(target):
        pl.semaphore_signal(barrier, inc=1, device_id=target, device_id_type=MESH)

    each_column(lambda to: greet((to, cy)))
    each_row(lambda to: greet((sx, to)))

    lane = lax.broadcasted_iota(jnp.int32, (8, FD), 1)
    sub = lax.broadcasted_iota(jnp.int32, (8, FD), 0)
    map_tile = jnp.zeros((8, FD), jnp.int32)
    for k in range(8):
        map_tile = jnp.where(sub == k, map_smem[0, 0, k], map_tile)
    map_tile = map_tile.astype(F32)
    live_x = jnp.logical_and(lane < cnt_smem[0, 0, 0], sx < gx_n - 1)
    live_y = jnp.logical_and(lane < cnt_smem[0, 0, 1], cy < gy_n - 1)
    for face, live in ((0, live_x), (1, live_y)):
        stat_v[face, 0:8, :] = map_tile
        stat_v[face, 8:16, :] = jnp.where(live, 1.0, 0.0).astype(F32)

    corner = (sx * gy_n + cy + corner_shift(sub, gy_n)).astype(F32)

    def basis_block(block, maps, modes):
        total = jnp.zeros((8, FD), F32)
        for k in range(8):
            total = total + jnp.where(corner == maps[k : k + 1, :], modes[k : k + 1, :], 0.0)
        hi = total.astype(BF16).astype(F32)
        lo = total - hi
        cols = slice(block * FD, (block + 1) * FD)
        oe_v[:, cols] = jnp.concatenate([hi, lo], axis=0).astype(BF16)
        oe2_v[:, cols] = jnp.concatenate([hi, hi, lo, lo], axis=0).astype(BF16)

    def own_live(face):
        return stat_v[face, 8:9, :]

    def all_live(block):
        face = block // 2
        if block % 2:
            return stat_v[face, 8:9, :]
        inside = (sx > 0) if face == 0 else (cy > 0)
        return jnp.where(inside, hs_v[face, 8:9, :], 0.0)

    lane_8 = lax.broadcasted_iota(jnp.int32, (8, LANES), 1)
    lane_4 = lax.broadcasted_iota(jnp.int32, (4, LANES), 1)

    def packed(tile):
        return jnp.where(lane_8 < R, tile, pltpu.roll(tile, 4, 0))[0:4]

    def unpacked(tile):
        other = pltpu.roll(tile, R, 1)
        return jnp.concatenate([jnp.where(lane_4 < R, tile, other), jnp.where(lane_4 < R, other, tile)], axis=0)

    def row_send(n, tile):
        g1_v[n, cy] = packed(tile)

        def send(to):
            pltpu.make_async_remote_copy(
                src_ref=g1_v.at[n, cy], dst_ref=g1_v.at[n, cy], send_sem=gssem.at[n, 0], recv_sem=grsem.at[n, 0],
                device_id=(sx, to), device_id_type=MESH,
            ).start()

        each_row(send)

    def column_send(n, source):
        def send(to):
            pltpu.make_async_remote_copy(
                src_ref=source(to), dst_ref=g2_v.at[n, sx], send_sem=gssem.at[n, 1], recv_sem=grsem.at[n, 1],
                device_id=(to, cy), device_id_type=MESH,
            ).start()

        each_column(send)

    def wait_all(ref, n, phase, recv):
        copy = pltpu.make_async_remote_copy(
            src_ref=ref, dst_ref=ref, send_sem=gssem.at[n, phase], recv_sem=grsem.at[n, phase],
            device_id=(sx, up_y), device_id_type=MESH,
        )
        if recv:
            copy.wait_recv()
        else:
            copy.wait_send()

    def wait_row(n):
        wait_all(g1_v.at[n, pl.ds(0, gy_n - 1)], n, 0, True)

    def wait_column(n):
        wait_all(g2_v.at[n, pl.ds(0, gx_n - 1)], n, 1, True)

    def tree(values):
        while len(values) > 1:
            values = [a + b for a, b in zip(values[::2], values[1::2])]
        return values[0]

    def restrict(xx, basis):
        t = lax.dot_general(basis, xx, (((1,), (1,)), ((), ())), preferred_element_type=F32)
        t = t[0:8] + t[8:16]
        return t + pltpu.roll(t, R, 1)

    lane_g = lax.broadcasted_iota(jnp.int32, (4 * gy_n, LANES), 1)
    lane_s = lax.broadcasted_iota(jnp.int32, (4 * gx_n, LANES), 1)

    def solve(n):
        wait_row(n)
        sums = g1_v[n].reshape(4 * gy_n, LANES)
        hi = sums.astype(BF16).astype(F32)
        lo = sums - hi
        terms = jnp.concatenate(
            [jnp.where(lane_g < R, hi, pltpu.roll(lo, R, 1)), jnp.where(lane_g < R, pltpu.roll(hi, R, 1), lo)], axis=0
        ).astype(BF16)
        part = jnp.dot(q_v[...], terms, preferred_element_type=F32)
        part = part + pltpu.roll(part, R, 1)
        part_v[n] = jnp.where(lane_s < R, part[: 4 * gx_n], part[4 * gx_n :]).reshape(gx_n, 4, LANES)
        g2_v[n, sx] = part_v[n, sx]
        column_send(n, lambda to: part_v.at[n, to])

    def solved(n):
        wait_column(n)
        return unpacked(tree([g2_v[n, i] for i in range(gx_n)]))

    def transposed(y):
        hi = y.astype(BF16).astype(F32)
        lo = y - hi
        terms = jnp.concatenate([hi, lo, hi, lo], axis=0)
        return jnp.transpose(terms)[:R].astype(BF16)

    def coarse_block(terms, ref, block):
        return jnp.dot(terms, ref[:, block * FD : (block + 1) * FD], preferred_element_type=F32)

    def gram(y):
        return tree([gram_v[j] * y[j : j + 1, :] for j in range(8)])

    targets = {0: (dn_x, cy), 1: (up_x, cy), 2: (sx, dn_y), 3: (sx, up_y)}

    def face_copy(op, block):
        return pltpu.make_async_remote_copy(
            src_ref=wsend.at[op, block], dst_ref=wrecv.at[op, block ^ 1],
            send_sem=wssem.at[op, block], recv_sem=wrsem.at[op, block ^ 1],
            device_id=targets[block], device_id_type=MESH,
        )

    def apply(op, xx, matrix, send=True):
        for block in range(4):
            out = jnp.dot(xx, matrix[:, block * FD : (block + 1) * FD], preferred_element_type=F32)
            wsend[op, block] = out[:R] + out[R:]
            if send:
                face_copy(op, block).start()

    def add_coarse(op, terms, order, send):
        for block in order:
            wsend[op, block] += coarse_block(terms, oef2_v, block)
            if block in send:
                face_copy(op, block).start()

    def collected(op, block):
        return jnp.where(all_live(block) > 0.5, wsend[op, block] - wrecv[op, block], 0.0)

    def wait_faces(op, blocks=(0, 1, 2, 3)):
        for block in blocks:
            face_copy(op, block ^ 1).wait_recv()

    loads[0].wait()
    loads[1].wait()
    r_own = []
    for face in range(2):
        cols = slice(face * FD, (face + 1) * FD)
        live = own_live(face)
        r_own.append(jnp.where(live > 0.5, f_v[:, cols], 0.0))
        basis_block(2 * face + 1, stat_v[face, 0:8, :], modes_v[:, cols] * live)
    basis_own = jnp.concatenate([oe_v[:, FD : 2 * FD], oe_v[:, 3 * FD :]], axis=1)
    first_sums = restrict(split_rows(jnp.concatenate(r_own, axis=1)), basis_own)

    pl.semaphore_wait(barrier, gy_n + gx_n - 2)

    row_send(0, first_sums)
    halo = []
    for face, target in ((0, (up_x, cy)), (1, (sx, up_y))):
        cols = pl.ds(face * FD, FD)
        for n, (src, dst) in enumerate((
            (stat_v.at[face], hs_v.at[face]),
            (modes_v.at[:, cols], hm_v.at[face]),
            (f_v.at[:, cols], hf_v.at[face]),
        )):
            copy = pltpu.make_async_remote_copy(
                src_ref=src, dst_ref=dst, send_sem=hsend.at[face, n], recv_sem=hrecv.at[face, n],
                device_id=target, device_id_type=MESH,
            )
            copy.start()
            halo.append(copy)

    loads[2].wait()
    row_q = lax.broadcasted_iota(jnp.int32, (8 * gx_n, LANES), 0)
    lane_q = lax.broadcasted_iota(jnp.int32, (8 * gx_n, LANES), 1)
    last_q = row_q >= 4 * gx_n
    row_q = jnp.where(last_q, row_q - 4 * gx_n, row_q)
    at = (row_q // 4) * gy_n + cy + corner_shift(lax.rem(row_q, 4) + jnp.where(last_q, 4, 0), gy_n) - lane_q
    pick = [jnp.where(at == g * LANES, 1.0, 0.0).astype(BF16) for g in range(corners // LANES)]
    to_column = lax.dot_general(
        jnp.concatenate(pick, axis=1), cinv_v[...], (((1,), (1,)), ((), ())), preferred_element_type=F32
    ).astype(BF16)
    row_p = lax.broadcasted_iota(jnp.int32, (8 * gy_n, LANES), 0)
    lane_p = lax.broadcasted_iota(jnp.int32, (8 * gy_n, LANES), 1)
    last_p = row_p >= 4 * gy_n
    row_p = jnp.where(last_p, row_p - 4 * gy_n, row_p)
    at = sx * gy_n + row_p // 4 + corner_shift(lax.rem(row_p, 4) + jnp.where(last_p, 4, 0), gy_n) - lane_p
    pick = [jnp.where(at == g * LANES, 1.0, 0.0).astype(BF16) for g in range(corners // LANES)]
    q_v[...] = lax.dot_general(
        to_column, jnp.concatenate(pick, axis=1), (((1,), (1,)), ((), ())), preferred_element_type=F32
    ).astype(BF16)

    halo[2].wait_recv()
    halo[5].wait_recv()
    halo[0].wait_recv()
    halo[3].wait_recv()
    x0 = jnp.concatenate(
        [
            -jnp.where(all_live(0) > 0.5, hf_v[0], 0.0),
            r_own[0],
            -jnp.where(all_live(2) > 0.5, hf_v[1], 0.0),
            r_own[1],
        ],
        axis=1,
    )
    loads[3].wait()
    apply(0, split_rows(x0), s_v)
    solve(0)

    halo[1].wait_recv()
    halo[4].wait_recv()
    for face in range(2):
        basis_block(2 * face, hs_v[face, 0:8, :], -(hm_v[face] * all_live(2 * face)))
    loads[4].wait()
    basis = oe_v[...]
    oef = jnp.dot(basis, a_v[...], preferred_element_type=F32)
    oef = oef[0:8] + oef[8:16]
    hi = oef.astype(BF16).astype(F32)
    lo = oef - hi
    oef_v[...] = jnp.concatenate([hi, lo], axis=0).astype(BF16)
    oef2_v[...] = jnp.concatenate([hi, hi, lo, lo], axis=0).astype(BF16)
    square = lax.dot_general(basis, oef_v[...], (((1,), (1,)), ((), ())), preferred_element_type=F32)
    square = square[0:8] + square[8:16]
    square = square[:, 0:8] + square[:, 8:16]
    for j in range(8):
        gram_v[j] = jnp.broadcast_to(square[:, j : j + 1], (8, LANES))

    def owned_dot(a, b):
        return jnp.sum(a[0] * b[0], axis=1, keepdims=True) + jnp.sum(a[1] * b[1], axis=1, keepdims=True)

    def owned(ref):
        return ref[:, FD : 2 * FD], ref[:, 3 * FD :]

    def images(op):
        return jnp.concatenate([wsend[op, block] for block in range(4)], axis=1)

    wait_faces(0)
    for block in range(4):
        xz_v[:, block * FD : (block + 1) * FD] = 0.25 * collected(0, block)
    xx = split_rows(xz_v[...])
    apply(1, xx, a_v, send=False)
    fine_sums = restrict(xx, oef_v[...])

    y = solved(0)
    next_sums = fine_sums + gram(y)
    row_send(1, next_sums)

    terms = transposed(y)
    add_coarse(1, terms, (0, 1, 2, 3), (0, 1, 2, 3))
    for block in range(4):
        xz_v[:, block * FD : (block + 1) * FD] += coarse_block(terms, oe2_v, block)
    w0 = images(1)
    gamma0 = owned_dot(r_own, owned(xz_v))
    delta0 = jnp.sum(xz_v[...] * w0, axis=1, keepdims=True)

    wait_faces(1)
    for block in range(4):
        xq_v[:, block * FD : (block + 1) * FD] = collected(1, block)
    xx = split_rows(xq_v[...])
    apply(2, xx, s_v)
    solve(1)
    image_sums = restrict(jnp.concatenate([xx[:, FD : 2 * FD], xx[:, 3 * FD :]], axis=1), basis_own)

    wait_faces(2)
    for block in range(4):
        xu_v[:, block * FD : (block + 1) * FD] = 0.25 * collected(2, block)
    xx = split_rows(xu_v[...])
    apply(3, xx, a_v, send=False)
    smoothed_sums = restrict(xx, oef_v[...])
    wv = images(3)
    sums = (
        gamma0,
        delta0,
        owned_dot(r_own, owned(xu_v)),
        owned_dot(owned(xq_v), owned(xu_v)),
        jnp.sum(xz_v[...] * wv + xu_v[...] * images(1), axis=1, keepdims=True),
        jnp.sum(xu_v[...] * wv, axis=1, keepdims=True),
    )
    lane_r = lax.broadcasted_iota(jnp.int32, (LANES, LANES), 1)
    tile = jnp.zeros((LANES, LANES), F32)
    for j, value in enumerate(sums):
        tile = jnp.where(lane_r == j, jnp.concatenate([value, value], axis=0), tile)
    fine_scalars = jnp.transpose(tile)[0:8]

    y = solved(1)
    sub_s = lax.broadcasted_iota(jnp.int32, (8, LANES), 0)
    coarse_scalars = jnp.zeros((8, LANES), F32)
    for j, factor in (
        (2, first_sums), (3, image_sums), (4, 2.0 * next_sums), (5, 2.0 * smoothed_sums + gram(y))
    ):
        coarse_scalars = jnp.where(sub_s == j, jnp.sum(y * factor, axis=0, keepdims=True), coarse_scalars)
    row_send(2, fine_scalars + coarse_scalars)

    terms = transposed(y)
    add_coarse(3, terms, (0, 2, 1, 3), (0, 2))
    for block in (1, 3):
        xu_v[:, block * FD : (block + 1) * FD] += coarse_block(terms, oe2_v, block)
    wait_row(2)
    g2_v[2, sx] = tree([g1_v[2, i] for i in range(gy_n)])
    column_send(2, lambda to: g2_v.at[2, sx])
    wait_faces(3, (1, 3))
    wait_column(2)
    scalars = unpacked(tree([g2_v[2, i] for i in range(gx_n)]))
    g0, d0, ru, qu, cross, uu = (scalars[j : j + 1] for j in range(6))
    alpha0 = g0 / d0
    g1 = alpha0 * (alpha0 * qu - ru)
    beta1 = 1.0 + g1 / g0
    d1 = beta1 * (beta1 * d0 - alpha0 * cross) + alpha0 * alpha0 * uu
    alpha1 = g1 / d1
    steps = jnp.where(sub_s == 0, alpha0 + alpha1 * beta1, alpha0 * alpha1)
    steps = jnp.transpose(steps)[:R]
    first, second = steps[:, 0:1], steps[:, 1:2]
    for face in range(2):
        block = 2 * face + 1
        cols = slice(face * FD, (face + 1) * FD)
        own = slice(block * FD, (block + 1) * FD)
        out_v[0, :, cols] = first * xz_v[:, own] - second * xu_v[:, own]
        out_v[1, :, cols] = r_own[face] - first * xq_v[:, own] + second * collected(3, block)

    for copy in halo:
        copy.wait_send()
    for op in range(4):
        for block in (0, 1, 2, 3) if op < 3 else (0, 2):
            face_copy(op, block).wait_send()
    for n in range(3):
        wait_all(g1_v.at[n, pl.ds(0, gy_n - 1)], n, 0, False)
        wait_all(g2_v.at[n, pl.ds(0, gx_n - 1)], n, 1, False)


def hand_out(both, x_out, r_out, sem):
    copies = [
        pltpu.make_async_copy(both.at[n], ref.at[0, 0], sem.at[n]) for n, ref in enumerate((x_out, r_out))
    ]
    for copy in copies:
        copy.start()
    for copy in copies:
        copy.wait()


def on_device(mesh_shape, forcing_terms, schur, flexibility, coarse_modes, coarse_map, face_slot_count, coarse_inverse):
    gx_n, gy_n = mesh_shape
    nb = 4 * FD
    hbm = pl.BlockSpec(memory_space=pl.ANY)
    smem = pl.BlockSpec(memory_space=pltpu.SMEM)
    vmem = pl.BlockSpec(memory_space=pltpu.VMEM)
    both = pl.pallas_call(
        functools.partial(kernel, gx_n, gy_n),
        out_shape=pltpu.VMEM((2, R, 2 * FD), F32),
        in_specs=[hbm, hbm, hbm, hbm, smem, smem, hbm],
        out_specs=vmem,
        scratch_shapes=[
            pltpu.VMEM((nb, nb), BF16),
            pltpu.VMEM((nb, nb), BF16),
            pltpu.VMEM(coarse_inverse.shape, BF16),
            pltpu.VMEM((R, 2 * FD), F32),
            pltpu.VMEM((8, 2 * FD), F32),
            pltpu.VMEM((2, 16, FD), F32),
            pltpu.VMEM((2, R, FD), F32),
            pltpu.VMEM((2, 8, FD), F32),
            pltpu.VMEM((2, 16, FD), F32),
            pltpu.VMEM((4, 4, R, FD), F32),
            pltpu.VMEM((4, 4, R, FD), F32),
            pltpu.VMEM((R, nb), F32),
            pltpu.VMEM((R, nb), F32),
            pltpu.VMEM((R, nb), F32),
            pltpu.VMEM((16, nb), BF16),
            pltpu.VMEM((32, nb), BF16),
            pltpu.VMEM((16, nb), BF16),
            pltpu.VMEM((32, nb), BF16),
            pltpu.VMEM((8, 8, LANES), F32),
            pltpu.VMEM((8 * gx_n, 8 * gy_n), BF16),
            pltpu.VMEM((3, gy_n, 4, LANES), F32),
            pltpu.VMEM((2, gx_n, 4, LANES), F32),
            pltpu.VMEM((3, gx_n, 4, LANES), F32),
            pltpu.SemaphoreType.DMA((5,)),
            pltpu.SemaphoreType.DMA((2, 3)),
            pltpu.SemaphoreType.DMA((2, 3)),
            pltpu.SemaphoreType.DMA((4, 4)),
            pltpu.SemaphoreType.DMA((4, 4)),
            pltpu.SemaphoreType.DMA((3, 2)),
            pltpu.SemaphoreType.DMA((3, 2)),
        ],
        compiler_params=pltpu.CompilerParams(
            collective_id=0, has_side_effects=True, vmem_limit_bytes=56 * 1024 * 1024
        ),
    )(forcing_terms, schur, flexibility, coarse_modes, coarse_map, face_slot_count, coarse_inverse)
    out = jax.ShapeDtypeStruct(forcing_terms.shape, F32)
    return pl.pallas_call(
        hand_out,
        out_shape=(out, out),
        in_specs=[vmem],
        out_specs=(hbm, hbm),
        scratch_shapes=[pltpu.SemaphoreType.DMA((2,))],
    )(both)


def solution(mesh):
    shape = (mesh.shape["gx"], mesh.shape["gy"])
    return jax.shard_map(
        functools.partial(on_device, shape),
        mesh=mesh,
        in_specs=(
            P("gx", "gy", None, None),
            P("gx", "gy", None, None),
            P("gx", "gy", None, None),
            P("gx", "gy", None, None),
            P("gx", "gy", None),
            P("gx", "gy", None),
            P(),
        ),
        out_specs=(P("gx", "gy", None, None), P("gx", "gy", None, None)),
        check_vma=False,
    )
```

```python
import functools

import jax
import jax.numpy as jnp
from jax import lax
from jax.experimental import pallas as pl
from jax.experimental.pallas import tpu as pltpu
from jax.sharding import PartitionSpec as P

MESH = pl.DeviceIdType.MESH
F32 = jnp.float32
BF16 = jnp.bfloat16
FD = 256
R = 64
LANES = 128
OFFSETS = ((0, 0), (0, 1), (1, 0), (1, 1), (-1, 0), (-1, 1), (0, -1), (1, -1))


def split_rows(x):
    hi = x.astype(BF16)
    lo = (x - hi.astype(F32)).astype(BF16)
    return jnp.concatenate([hi, lo], axis=0)


def corner_shift(j, columns):
    shift = jnp.zeros_like(j)
    for n, (a, b) in enumerate(OFFSETS):
        shift = jnp.where(j == n, a * columns + b, shift)
    return shift


def kernel(
    gx_n, gy_n,
    f_hbm, s_hbm, a_hbm, modes_hbm, map_smem, cnt_smem, cinv_hbm,
    out_v,
    s_v, a_v, cinv_v, f_v, modes_v,
    stat_v, fs_v, hf_v, hm_v, hs_v,
    wsend, wrecv, wlast, wshort, xz_v, xq_v, xu_v, oe_v, oe2_v, oef_v, oef2_v, gram_v, q_v,
    g1_v, part_v, g2_v,
    lsem, hsend, hrecv, wssem, wrsem, gssem, grsem, met_sem,
):
    sx = lax.axis_index("gx")
    cy = lax.axis_index("gy")
    corners = gx_n * gy_n
    up_x = lax.rem(sx + 1, gx_n)
    dn_x = lax.rem(sx + gx_n - 1, gx_n)
    up_y = lax.rem(cy + 1, gy_n)
    dn_y = lax.rem(cy + gy_n - 1, gy_n)

    loads = [
        pltpu.make_async_copy(f_hbm.at[0, 0], f_v, lsem.at[0]),
        pltpu.make_async_copy(modes_hbm.at[0, 0], modes_v, lsem.at[1]),
        pltpu.make_async_copy(cinv_hbm, cinv_v, lsem.at[2]),
        pltpu.make_async_copy(s_hbm.at[0, 0], s_v, lsem.at[3]),
        pltpu.make_async_copy(a_hbm.at[0, 0], a_v, lsem.at[4]),
    ]
    for load in loads:
        load.start()

    def each_row(send):
        half = gy_n // 2
        send(lax.rem(cy + half, gy_n))

        def pair(i, carry):
            send(lax.rem(cy + half + i, gy_n))
            send(lax.rem(cy + half - i, gy_n))
            return carry

        lax.fori_loop(1, half, pair, 0)

    x_n, z_n = 4, gx_n // 4
    x_at, z_at = sx // z_n, lax.rem(sx, z_n)

    def each_z(send):
        half = z_n // 2
        send(x_at * z_n + lax.rem(z_at + half, z_n))

        def pair(i, carry):
            send(x_at * z_n + lax.rem(z_at + half + i, z_n))
            send(x_at * z_n + lax.rem(z_at + half - i, z_n))
            return carry

        lax.fori_loop(1, half, pair, 0)

    def each_x(send):
        for dx in (2, 1, 3):
            send(lax.rem(x_at + dx, x_n) * z_n + z_at)

    def each_column(send):
        half = z_n // 2

        def level(dz, shifts=(2, 1, 3, 0)):
            z_to = lax.rem(z_at + dz, z_n)
            for dx in shifts:
                send(lax.rem(x_at + dx, x_n) * z_n + z_to)

        level(half)

        def pair(i, carry):
            level(half + i)
            level(half - i)
            return carry

        lax.fori_loop(1, half, pair, 0)
        level(0, (2, 1, 3))

    barrier = pltpu.get_barrier_semaphore()

    def greet(target):
        pl.semaphore_signal(barrier, inc=1, device_id=target, device_id_type=MESH)

    each_z(lambda to: greet((to, cy)))
    each_row(lambda to: greet((sx, to)))
    each_x(lambda to: greet((to, cy)))
    greet((up_x, cy))
    greet((dn_x, cy))

    lane = lax.broadcasted_iota(jnp.int32, (8, FD), 1)
    sub = lax.broadcasted_iota(jnp.int32, (8, FD), 0)
    map_tile = jnp.zeros((8, FD), jnp.int32)
    for k in range(8):
        map_tile = jnp.where(sub == k, map_smem[0, 0, k], map_tile)
    map_tile = map_tile.astype(F32)
    live_x = jnp.logical_and(lane < cnt_smem[0, 0, 0], sx < gx_n - 1)
    live_y = jnp.logical_and(lane < cnt_smem[0, 0, 1], cy < gy_n - 1)
    for face, live in ((0, live_x), (1, live_y)):
        stat_v[face, 0:8, :] = map_tile
        stat_v[face, 8:16, :] = jnp.where(live, 1.0, 0.0).astype(F32)

    corner = (sx * gy_n + cy + corner_shift(sub, gy_n)).astype(F32)

    def basis_block(block, maps, modes):
        total = jnp.zeros((8, FD), F32)
        for k in range(8):
            total = total + jnp.where(corner == maps[k : k + 1, :], modes[k : k + 1, :], 0.0)
        hi = total.astype(BF16).astype(F32)
        lo = total - hi
        cols = slice(block * FD, (block + 1) * FD)
        oe_v[:, cols] = jnp.concatenate([hi, lo], axis=0).astype(BF16)
        oe2_v[:, cols] = jnp.concatenate([hi, hi, lo, lo], axis=0).astype(BF16)

    def own_live(face):
        return stat_v[face, 8:9, :]

    def all_live(block):
        face = block // 2
        if block % 2:
            return stat_v[face, 8:9, :]
        inside = (sx > 0) if face == 0 else (cy > 0)
        return jnp.where(inside, hs_v[face, 8:9, :], 0.0)

    lane_8 = lax.broadcasted_iota(jnp.int32, (8, LANES), 1)
    lane_4 = lax.broadcasted_iota(jnp.int32, (4, LANES), 1)

    def packed(tile):
        return jnp.where(lane_8 < R, tile, pltpu.roll(tile, 4, 0))[0:4]

    def unpacked(tile):
        other = pltpu.roll(tile, R, 1)
        return jnp.concatenate([jnp.where(lane_4 < R, tile, other), jnp.where(lane_4 < R, other, tile)], axis=0)

    def row_send(n, tile):
        g1_v[n, cy] = packed(tile)

        def send(to):
            pltpu.make_async_remote_copy(
                src_ref=g1_v.at[n, cy], dst_ref=g1_v.at[n, cy], send_sem=gssem.at[n, 0], recv_sem=grsem.at[n, 0],
                device_id=(sx, to), device_id_type=MESH,
            ).start()

        each_row(send)

    def column_send(n, source):
        def send(to):
            pltpu.make_async_remote_copy(
                src_ref=source(to), dst_ref=g2_v.at[n, sx], send_sem=gssem.at[n, 1], recv_sem=grsem.at[n, 1],
                device_id=(to, cy), device_id_type=MESH,
            ).start()

        each_column(send)

    def wait_all(ref, n, phase, recv):
        copy = pltpu.make_async_remote_copy(
            src_ref=ref, dst_ref=ref, send_sem=gssem.at[n, phase], recv_sem=grsem.at[n, phase],
            device_id=(sx, up_y), device_id_type=MESH,
        )
        if recv:
            copy.wait_recv()
        else:
            copy.wait_send()

    def wait_row(n):
        wait_all(g1_v.at[n, pl.ds(0, gy_n - 1)], n, 0, True)

    def wait_column(n):
        wait_all(g2_v.at[n, pl.ds(0, gx_n - 1)], n, 1, True)

    def tree(values):
        while len(values) > 1:
            values = [a + b for a, b in zip(values[::2], values[1::2])]
        return values[0]

    def restrict(xx, basis):
        t = lax.dot_general(basis, xx, (((1,), (1,)), ((), ())), preferred_element_type=F32)
        t = t[0:8] + t[8:16]
        return t + pltpu.roll(t, R, 1)

    lane_g = lax.broadcasted_iota(jnp.int32, (4 * gy_n, LANES), 1)
    lane_s = lax.broadcasted_iota(jnp.int32, (4 * gx_n, LANES), 1)

    def solve(n):
        wait_row(n)
        sums = g1_v[n].reshape(4 * gy_n, LANES)
        hi = sums.astype(BF16).astype(F32)
        lo = sums - hi
        terms = jnp.concatenate(
            [jnp.where(lane_g < R, hi, pltpu.roll(lo, R, 1)), jnp.where(lane_g < R, pltpu.roll(hi, R, 1), lo)], axis=0
        ).astype(BF16)
        part = jnp.dot(q_v[...], terms, preferred_element_type=F32)
        part = part + pltpu.roll(part, R, 1)
        part_v[n] = jnp.where(lane_s < R, part[: 4 * gx_n], part[4 * gx_n :]).reshape(gx_n, 4, LANES)
        g2_v[n, sx] = part_v[n, sx]
        column_send(n, lambda to: part_v.at[n, to])

    def solved(n):
        wait_column(n)
        return unpacked(tree([g2_v[n, i] for i in range(gx_n)]))

    def transposed(y):
        hi = y.astype(BF16).astype(F32)
        lo = y - hi
        terms = jnp.concatenate([hi, lo, hi, lo], axis=0)
        return jnp.transpose(terms)[:R].astype(BF16)

    def coarse_block(terms, ref, block):
        return jnp.dot(terms, ref[:, block * FD : (block + 1) * FD], preferred_element_type=F32)

    def gram(y):
        return tree([gram_v[j] * y[j : j + 1, :] for j in range(8)])

    targets = {0: (dn_x, cy), 1: (up_x, cy), 2: (sx, dn_y), 3: (sx, up_y)}

    def face_copy(op, block):
        return pltpu.make_async_remote_copy(
            src_ref=wshort.at[op, block] if op < 3 else wsend.at[op, block],
            dst_ref=wrecv.at[op, block ^ 1] if op < 3 else wlast.at[block ^ 1],
            send_sem=wssem.at[op, block], recv_sem=wrsem.at[op, block ^ 1],
            device_id=targets[block], device_id_type=MESH,
        )

    def send_face(op, block):
        if op < 3:
            wshort[op, block] = wsend[op, block].astype(BF16)
        face_copy(op, block).start()

    def apply(op, xx, matrix, send=True):
        for block in range(4):
            out = jnp.dot(xx, matrix[:, block * FD : (block + 1) * FD], preferred_element_type=F32)
            wsend[op, block] = out[:R] + out[R:]
            if send:
                send_face(op, block)

    def add_coarse(op, terms, order, send):
        for block in order:
            wsend[op, block] += coarse_block(terms, oef2_v, block)
            if block in send:
                send_face(op, block)

    def collected(op, block):
        return jnp.where(all_live(block) > 0.5, wsend[op, block] - (wrecv[op, block].astype(F32) if op < 3 else wlast[block]), 0.0)

    def wait_faces(op, blocks=(0, 1, 2, 3)):
        for block in blocks:
            face_copy(op, block ^ 1).wait_recv()

    loads[0].wait()
    loads[1].wait()
    r_own = []
    for face in range(2):
        cols = slice(face * FD, (face + 1) * FD)
        live = own_live(face)
        r_own.append(jnp.where(live > 0.5, f_v[:, cols], 0.0))
        fs_v[face] = r_own[face].astype(BF16)
        basis_block(2 * face + 1, stat_v[face, 0:8, :], modes_v[:, cols] * live)
    basis_own = jnp.concatenate([oe_v[:, FD : 2 * FD], oe_v[:, 3 * FD :]], axis=1)
    first_sums = restrict(split_rows(jnp.concatenate(r_own, axis=1)), basis_own)

    pl.semaphore_wait(barrier, gy_n + z_n + x_n - 1)

    row_send(0, first_sums)
    each_x(lambda to: pl.semaphore_signal(met_sem, inc=1, device_id=(to, cy), device_id_type=MESH))
    halo = []
    for face, target in ((0, (up_x, cy)), (1, (sx, up_y))):
        cols = pl.ds(face * FD, FD)
        for n, (src, dst) in enumerate((
            (stat_v.at[face], hs_v.at[face]),
            (modes_v.at[:, cols], hm_v.at[face]),
            (fs_v.at[face], hf_v.at[face]),
        )):
            copy = pltpu.make_async_remote_copy(
                src_ref=src, dst_ref=dst, send_sem=hsend.at[face, n], recv_sem=hrecv.at[face, n],
                device_id=target, device_id_type=MESH,
            )
            copy.start()
            halo.append(copy)

    loads[2].wait()
    row_q = lax.broadcasted_iota(jnp.int32, (8 * gx_n, LANES), 0)
    lane_q = lax.broadcasted_iota(jnp.int32, (8 * gx_n, LANES), 1)
    last_q = row_q >= 4 * gx_n
    row_q = jnp.where(last_q, row_q - 4 * gx_n, row_q)
    at = (row_q // 4) * gy_n + cy + corner_shift(lax.rem(row_q, 4) + jnp.where(last_q, 4, 0), gy_n) - lane_q
    pick = [jnp.where(at == g * LANES, 1.0, 0.0).astype(BF16) for g in range(corners // LANES)]
    to_column = lax.dot_general(
        jnp.concatenate(pick, axis=1), cinv_v[...], (((1,), (1,)), ((), ())), preferred_element_type=F32
    ).astype(BF16)
    row_p = lax.broadcasted_iota(jnp.int32, (8 * gy_n, LANES), 0)
    lane_p = lax.broadcasted_iota(jnp.int32, (8 * gy_n, LANES), 1)
    last_p = row_p >= 4 * gy_n
    row_p = jnp.where(last_p, row_p - 4 * gy_n, row_p)
    at = sx * gy_n + row_p // 4 + corner_shift(lax.rem(row_p, 4) + jnp.where(last_p, 4, 0), gy_n) - lane_p
    pick = [jnp.where(at == g * LANES, 1.0, 0.0).astype(BF16) for g in range(corners // LANES)]
    q_v[...] = lax.dot_general(
        to_column, jnp.concatenate(pick, axis=1), (((1,), (1,)), ((), ())), preferred_element_type=F32
    ).astype(BF16)

    halo[2].wait_recv()
    halo[5].wait_recv()
    halo[0].wait_recv()
    halo[3].wait_recv()
    x0 = jnp.concatenate(
        [
            -jnp.where(all_live(0) > 0.5, hf_v[0].astype(F32), 0.0),
            r_own[0],
            -jnp.where(all_live(2) > 0.5, hf_v[1].astype(F32), 0.0),
            r_own[1],
        ],
        axis=1,
    )
    loads[3].wait()
    apply(0, split_rows(x0), s_v)
    pl.semaphore_wait(met_sem, x_n - 1)
    solve(0)

    halo[1].wait_recv()
    halo[4].wait_recv()
    for face in range(2):
        basis_block(2 * face, hs_v[face, 0:8, :], -(hm_v[face] * all_live(2 * face)))
    loads[4].wait()
    basis = oe_v[...]
    oef = jnp.dot(basis, a_v[...], preferred_element_type=F32)
    oef = oef[0:8] + oef[8:16]
    hi = oef.astype(BF16).astype(F32)
    lo = oef - hi
    oef_v[...] = jnp.concatenate([hi, lo], axis=0).astype(BF16)
    oef2_v[...] = jnp.concatenate([hi, hi, lo, lo], axis=0).astype(BF16)
    square = lax.dot_general(basis, oef_v[...], (((1,), (1,)), ((), ())), preferred_element_type=F32)
    square = square[0:8] + square[8:16]
    square = square[:, 0:8] + square[:, 8:16]
    for j in range(8):
        gram_v[j] = jnp.broadcast_to(square[:, j : j + 1], (8, LANES))

    def owned_dot(a, b):
        return jnp.sum(a[0] * b[0], axis=1, keepdims=True) + jnp.sum(a[1] * b[1], axis=1, keepdims=True)

    def owned(ref):
        return ref[:, FD : 2 * FD], ref[:, 3 * FD :]

    def images(op):
        return jnp.concatenate([wsend[op, block] for block in range(4)], axis=1)

    wait_faces(0)
    for block in range(4):
        xz_v[:, block * FD : (block + 1) * FD] = 0.25 * collected(0, block)
    xx = split_rows(xz_v[...])
    apply(1, xx, a_v, send=False)
    fine_sums = restrict(xx, oef_v[...])

    y = solved(0)
    next_sums = fine_sums + gram(y)
    row_send(1, next_sums)

    terms = transposed(y)
    add_coarse(1, terms, (0, 1, 2, 3), (0, 1, 2, 3))
    for block in range(4):
        xz_v[:, block * FD : (block + 1) * FD] += coarse_block(terms, oe2_v, block)
    w0 = images(1)
    gamma0 = owned_dot(r_own, owned(xz_v))
    delta0 = jnp.sum(xz_v[...] * w0, axis=1, keepdims=True)

    wait_faces(1)
    for block in range(4):
        xq_v[:, block * FD : (block + 1) * FD] = collected(1, block)
    xx = split_rows(xq_v[...])
    apply(2, xx, s_v)
    solve(1)
    image_sums = restrict(jnp.concatenate([xx[:, FD : 2 * FD], xx[:, 3 * FD :]], axis=1), basis_own)

    wait_faces(2)
    for block in range(4):
        xu_v[:, block * FD : (block + 1) * FD] = 0.25 * collected(2, block)
    xx = split_rows(xu_v[...])
    apply(3, xx, a_v, send=False)
    smoothed_sums = restrict(xx, oef_v[...])
    wv = images(3)
    sums = (
        gamma0,
        delta0,
        owned_dot(r_own, owned(xu_v)),
        owned_dot(owned(xq_v), owned(xu_v)),
        jnp.sum(xz_v[...] * wv + xu_v[...] * images(1), axis=1, keepdims=True),
        jnp.sum(xu_v[...] * wv, axis=1, keepdims=True),
    )
    lane_r = lax.broadcasted_iota(jnp.int32, (LANES, LANES), 1)
    tile = jnp.zeros((LANES, LANES), F32)
    for j, value in enumerate(sums):
        tile = jnp.where(lane_r == j, jnp.concatenate([value, value], axis=0), tile)
    fine_scalars = jnp.transpose(tile)[0:8]

    y = solved(1)
    sub_s = lax.broadcasted_iota(jnp.int32, (8, LANES), 0)
    coarse_scalars = jnp.zeros((8, LANES), F32)
    for j, factor in (
        (2, first_sums), (3, image_sums), (4, 2.0 * next_sums), (5, 2.0 * smoothed_sums + gram(y))
    ):
        coarse_scalars = jnp.where(sub_s == j, jnp.sum(y * factor, axis=0, keepdims=True), coarse_scalars)
    row_send(2, fine_scalars + coarse_scalars)

    terms = transposed(y)
    add_coarse(3, terms, (0, 2, 1, 3), (0, 2))
    for block in (1, 3):
        xu_v[:, block * FD : (block + 1) * FD] += coarse_block(terms, oe2_v, block)
    wait_row(2)
    g2_v[2, sx] = tree([g1_v[2, i] for i in range(gy_n)])
    column_send(2, lambda to: g2_v.at[2, sx])
    wait_faces(3, (1, 3))
    wait_column(2)
    scalars = unpacked(tree([g2_v[2, i] for i in range(gx_n)]))
    g0, d0, ru, qu, cross, uu = (scalars[j : j + 1] for j in range(6))
    alpha0 = g0 / d0
    g1 = alpha0 * (alpha0 * qu - ru)
    beta1 = 1.0 + g1 / g0
    d1 = beta1 * (beta1 * d0 - alpha0 * cross) + alpha0 * alpha0 * uu
    alpha1 = g1 / d1
    steps = jnp.where(sub_s == 0, alpha0 + alpha1 * beta1, alpha0 * alpha1)
    steps = jnp.transpose(steps)[:R]
    first, second = steps[:, 0:1], steps[:, 1:2]
    for face in range(2):
        block = 2 * face + 1
        cols = slice(face * FD, (face + 1) * FD)
        own = slice(block * FD, (block + 1) * FD)
        out_v[0, :, cols] = first * xz_v[:, own] - second * xu_v[:, own]
        out_v[1, :, cols] = r_own[face] - first * xq_v[:, own] + second * collected(3, block)

    for copy in halo:
        copy.wait_send()
    for op in range(4):
        for block in (0, 1, 2, 3) if op < 3 else (0, 2):
            face_copy(op, block).wait_send()
    for n in range(3):
        wait_all(g1_v.at[n, pl.ds(0, gy_n - 1)], n, 0, False)
        wait_all(g2_v.at[n, pl.ds(0, gx_n - 1)], n, 1, False)


def hand_out(both, x_out, r_out, sem):
    copies = [
        pltpu.make_async_copy(both.at[n], ref.at[0, 0], sem.at[n]) for n, ref in enumerate((x_out, r_out))
    ]
    for copy in copies:
        copy.start()
    for copy in copies:
        copy.wait()


def on_device(mesh_shape, forcing_terms, schur, flexibility, coarse_modes, coarse_map, face_slot_count, coarse_inverse):
    gx_n, gy_n = mesh_shape
    nb = 4 * FD
    hbm = pl.BlockSpec(memory_space=pl.ANY)
    smem = pl.BlockSpec(memory_space=pltpu.SMEM)
    vmem = pl.BlockSpec(memory_space=pltpu.VMEM)
    both = pl.pallas_call(
        functools.partial(kernel, gx_n, gy_n),
        out_shape=pltpu.VMEM((2, R, 2 * FD), F32),
        in_specs=[hbm, hbm, hbm, hbm, smem, smem, hbm],
        out_specs=vmem,
        scratch_shapes=[
            pltpu.VMEM((nb, nb), BF16),
            pltpu.VMEM((nb, nb), BF16),
            pltpu.VMEM(coarse_inverse.shape, BF16),
            pltpu.VMEM((R, 2 * FD), F32),
            pltpu.VMEM((8, 2 * FD), F32),
            pltpu.VMEM((2, 16, FD), F32),
            pltpu.VMEM((2, R, FD), BF16),
            pltpu.VMEM((2, R, FD), BF16),
            pltpu.VMEM((2, 8, FD), F32),
            pltpu.VMEM((2, 16, FD), F32),
            pltpu.VMEM((4, 4, R, FD), F32),
            pltpu.VMEM((3, 4, R, FD), BF16),
            pltpu.VMEM((4, R, FD), F32),
            pltpu.VMEM((3, 4, R, FD), BF16),
            pltpu.VMEM((R, nb), F32),
            pltpu.VMEM((R, nb), F32),
            pltpu.VMEM((R, nb), F32),
            pltpu.VMEM((16, nb), BF16),
            pltpu.VMEM((32, nb), BF16),
            pltpu.VMEM((16, nb), BF16),
            pltpu.VMEM((32, nb), BF16),
            pltpu.VMEM((8, 8, LANES), F32),
            pltpu.VMEM((8 * gx_n, 8 * gy_n), BF16),
            pltpu.VMEM((3, gy_n, 4, LANES), F32),
            pltpu.VMEM((2, gx_n, 4, LANES), F32),
            pltpu.VMEM((3, gx_n, 4, LANES), F32),
            pltpu.SemaphoreType.DMA((5,)),
            pltpu.SemaphoreType.DMA((2, 3)),
            pltpu.SemaphoreType.DMA((2, 3)),
            pltpu.SemaphoreType.DMA((4, 4)),
            pltpu.SemaphoreType.DMA((4, 4)),
            pltpu.SemaphoreType.DMA((3, 2)),
            pltpu.SemaphoreType.DMA((3, 2)),
            pltpu.SemaphoreType.REGULAR,
        ],
        compiler_params=pltpu.CompilerParams(
            collective_id=0, has_side_effects=True, vmem_limit_bytes=56 * 1024 * 1024
        ),
    )(forcing_terms, schur, flexibility, coarse_modes, coarse_map, face_slot_count, coarse_inverse)
    out = jax.ShapeDtypeStruct(forcing_terms.shape, F32)
    return pl.pallas_call(
        hand_out,
        out_shape=(out, out),
        in_specs=[vmem],
        out_specs=(hbm, hbm),
        scratch_shapes=[pltpu.SemaphoreType.DMA((2,))],
    )(pltpu.with_memory_space_constraint(both, pltpu.VMEM))


def solution(mesh):
    shape = (mesh.shape["gx"], mesh.shape["gy"])
    return jax.shard_map(
        functools.partial(on_device, shape),
        mesh=mesh,
        in_specs=(
            P("gx", "gy", None, None),
            P("gx", "gy", None, None),
            P("gx", "gy", None, None),
            P("gx", "gy", None, None),
            P("gx", "gy", None),
            P("gx", "gy", None),
            P(),
        ),
        out_specs=(P("gx", "gy", None, None), P("gx", "gy", None, None)),
        check_vma=False,
    )
```
